32 devices in a mesh: segment: 4 (over y, core), dp: 8 (over z, x).
Axes of the slice: x: 2, y: 2, z: 4, core: 2. Of those that a mesh axis runs over, the one named last changes fastest.
Arguments:
- student_in: bfloat16 [4, 16, 8, 8, 512], P(None, 'dp'), may hold values from -6 to 6
- teacher_in: bfloat16 [4, 16, 8, 8, 512], P(None, 'dp'), may hold values from -6 to 6
- out_grad: bfloat16 [4, 16, 8, 8, 512], P(None, 'dp'), may hold values from -6 to 6
- student_params: float32 [4, 2621440], P('segment', 'dp'), may hold values from -0.5625 to 0.5625, as said below
- teacher_params: float32 [4, 2621440], P('segment', 'dp'), may hold values from -0.5625 to 0.5625, as said below
Outputs:
- teacher_acts: bfloat16 [4, 4, 16, 8, 8, 512], P('segment', None, 'dp')
- input_grads: bfloat16 [4, 4, 16, 8, 8, 512], P('segment', None, 'dp')
- param_grads: float32 [4, 2621440], P('segment', 'dp')
- teacher_new: float32 [4, 2621440], P('segment', 'dp')
The draws below stay inside these ranges and needn't reach their ends.
Inputs may be any that keep to these rules, and one draw needn't show every extreme that they name: `student_params`: independent entries of both signs. `teacher_params`: independent entries of both signs.
All inputs are finite; a program needn't handle non-finite values.
Results may differ from the reference program's by a relative error of at most 0.03.
Values may be sent and summed in bfloat16 or wider, within the bound.
A program may use at most 128 MiB of HBM per device.

```python
import jax
import jax.numpy as jnp
from jax import lax

C = 512
SE = 256
SIDE = 8
MICRO = 4
L = 4
IMGS = 16
PARAMS = 2621440


def param_rows(key):
    position = jnp.arange(PARAMS)
    tap_count = 9 * C * C
    scale = jnp.where(position < tap_count, (9.0 * C) ** (-0.5), jnp.where(position < tap_count + C * SE, 2.0 * C ** (-0.5), 3.0 * SE ** (-0.5)))
    base = jax.random.truncated_normal(key, -3.0, 3.0, (L, PARAMS), jnp.float32)
    return base * scale[None, :]


def draw_student_params(key, part):
    return param_rows(jax.random.fold_in(key, 11))


def draw_teacher_params(key, part):
    return param_rows(jax.random.fold_in(key, 23))


def levels(own_key, shape, pieces, low, top_value):
    factor_of = 1.0
    for dim, shards_of in pieces:
        draws = jax.random.uniform(jax.random.fold_in(jax.random.fold_in(own_key, 6), dim), (shards_of,), jnp.float32, low / len(pieces), top_value / len(pieces))
        factor_of = factor_of * jnp.repeat(jnp.exp(draws), shape[dim] // shards_of).reshape((-1,) + (1,) * (len(shape) - 1 - dim))
    return factor_of


def normal_values(rng, shape, width, bound, pieces=(), kind=jnp.bfloat16):
    values = width * jax.random.normal(rng, shape, jnp.float32)
    if pieces:
        values = values * levels(rng, shape, pieces, -0.22, 0.18)
    return jnp.clip(values, -bound, bound).astype(kind)


def setup_inputs(seed: int = 0) -> dict:
    seeds = jax.random.split(jax.random.key(seed), 6)
    student_in = normal_values(seeds[0], (MICRO, IMGS, SIDE, SIDE, C), 1.0, 6.0, ((1, 8),))
    teacher_in = normal_values(seeds[1], (MICRO, IMGS, SIDE, SIDE, C), 1.0, 6.0, ((1, 8),))
    out_grad = normal_values(seeds[2], (MICRO, IMGS, SIDE, SIDE, C), 1.0, 6.0, ((1, 8),))
    student_params = draw_student_params(jax.random.fold_in(seeds[5], 71), 0)
    teacher_params = draw_teacher_params(jax.random.fold_in(seeds[5], 71), 0)
    return {"student_in": student_in, "teacher_in": teacher_in, "out_grad": out_grad, "student_params": student_params, "teacher_params": teacher_params}


ema_keep = 0.99
step_rate = 0.001

def split_row(row, channels, squeeze):
    tap_count = 9 * channels * channels
    kernel = row[:tap_count].reshape(9 * channels, channels)
    reduce_w = row[tap_count:tap_count + channels * squeeze].reshape(channels, squeeze)
    expand_w = row[tap_count + channels * squeeze:].reshape(squeeze, channels)
    return (kernel, reduce_w, expand_w)

def gated_block(images, kernel, reduce_w, expand_w):
    side_h, side_w, channels = (images.shape[1], images.shape[2], images.shape[3])
    padded = jnp.pad(images, ((0, 0), (1, 1), (1, 1), (0, 0)))
    columns = jnp.concatenate([padded[:, row_off:row_off + side_h, col_off:col_off + side_w, :] for row_off in range(3) for col_off in range(3)], axis=-1)
    mixed_sum = jnp.dot(columns.reshape(-1, 9 * channels), kernel, preferred_element_type=jnp.float32)
    active = jax.nn.silu(mixed_sum).reshape(images.shape)
    pooled = lax.optimization_barrier(jnp.mean(active, axis=(1, 2))).astype(jnp.bfloat16)
    hidden = jax.nn.silu(jnp.dot(pooled, reduce_w, preferred_element_type=jnp.float32)).astype(jnp.bfloat16)
    gate_val = jax.nn.sigmoid(jnp.dot(hidden, expand_w, preferred_element_type=jnp.float32))
    return (images.astype(jnp.float32) + active * gate_val[:, None, None, :]).astype(jnp.bfloat16)

def one_image(picture, kernel, reduce_w, expand_w, cotangent):

    def local_block(inputs_one, kern_one, red_one, exp_one):
        return gated_block(inputs_one[None], kern_one, red_one, exp_one)[0]
    primal_out, pull_back = jax.vjp(local_block, picture, kernel, reduce_w, expand_w)
    return pull_back(cotangent.astype(primal_out.dtype))

def reference(student_in, teacher_in, out_grad, student_params, teacher_params):
    student_in = student_in.astype(jnp.bfloat16)
    teacher_in = teacher_in.astype(jnp.bfloat16)
    out_grad = out_grad.astype(jnp.bfloat16)
    student_params = student_params.astype(jnp.float32)
    teacher_params = teacher_params.astype(jnp.float32)
    micro_count, image_count = (student_in.shape[0], student_in.shape[1])
    channels = student_in.shape[-1]
    flat_shape = (micro_count * image_count,) + student_in.shape[2:]
    current = student_in
    teacher_now = teacher_in
    saved = []
    teacher_list = []
    weights_list = []
    for layer_idx in range(L):
        student_w = split_row(student_params[layer_idx].astype(jnp.bfloat16), channels, SE)
        teacher_w = split_row(teacher_params[layer_idx].astype(jnp.bfloat16), channels, SE)
        weights_list.append(student_w)
        saved.append(current)
        current = lax.map(lambda group: gated_block(group, *student_w), current)
        teacher_now = lax.map(lambda group: gated_block(group, *teacher_w), teacher_now)
        teacher_list.append(teacher_now)
    cotangent = out_grad.reshape(flat_shape)
    grads_list = [None] * L
    rows_list = [None] * L
    for layer_idx in range(L - 1, -1, -1):
        kernel, reduce_w, expand_w = weights_list[layer_idx]

        def per_image(totals, inputs_pair):
            picture, cot_one = inputs_pair
            d_in, d_kern, d_red, d_exp = one_image(picture, kernel, reduce_w, expand_w, cot_one)
            return ((totals[0] + d_kern.astype(jnp.float32), totals[1] + d_red.astype(jnp.float32), totals[2] + d_exp.astype(jnp.float32)), d_in.astype(jnp.bfloat16))
        zero_sums = (jnp.zeros(kernel.shape, jnp.float32), jnp.zeros(reduce_w.shape, jnp.float32), jnp.zeros(expand_w.shape, jnp.float32))
        totals, cotangent = lax.scan(per_image, zero_sums, (saved[layer_idx].reshape(flat_shape), cotangent))
        grads_list[layer_idx] = cotangent.reshape(student_in.shape)
        rows_list[layer_idx] = jnp.concatenate([totals[0].reshape(-1), totals[1].reshape(-1), totals[2].reshape(-1)])
    param_grads = jnp.stack(rows_list)
    teacher_new = ema_keep * teacher_params + (1.0 - ema_keep) * (student_params - step_rate * param_grads)
    return (jnp.stack(teacher_list), jnp.stack(grads_list), param_grads, teacher_new)
```

```python
import jax
import jax.numpy as jnp
from jax import lax
from jax.sharding import PartitionSpec as P

SE = 256


ema_keep = 0.99
step_rate = 0.001


def shift(array, axis, by):
    peers = lax.axis_size(axis)
    pairs = [(i, i + by) for i in range(peers) if 0 <= i + by < peers]
    return lax.ppermute(array, axis, pairs)


def split_rows(rows, channels, squeeze):
    taps = 9 * channels
    kernel = rows[:taps]
    pair = channels * squeeze // channels
    reduce_w = rows[taps : taps + pair].reshape(channels, squeeze)
    expand_w = rows[taps + pair :].reshape(squeeze, channels)
    return (kernel, reduce_w, expand_w)


def unfold(images):
    side_h, side_w, channels = images.shape[1:]
    padded = jnp.pad(images, ((0, 0), (1, 1), (1, 1), (0, 0)))
    columns = jnp.concatenate(
        [
            padded[:, row_off : row_off + side_h, col_off : col_off + side_w, :]
            for row_off in range(3)
            for col_off in range(3)
        ],
        axis=-1,
    )
    return columns.reshape(-1, 9 * channels)


def forward(images, kernel, reduce_w, expand_w):
    mixed = jnp.dot(unfold(images), kernel, preferred_element_type=jnp.float32)
    mixed = mixed.reshape(images.shape)
    active = jax.nn.silu(mixed)
    pooled = jnp.mean(active, axis=(1, 2)).astype(jnp.bfloat16)
    squeezed = jnp.dot(pooled, reduce_w, preferred_element_type=jnp.float32)
    hidden = jax.nn.silu(squeezed).astype(jnp.bfloat16)
    gate = jax.nn.sigmoid(jnp.dot(hidden, expand_w, preferred_element_type=jnp.float32))
    out = (images.astype(jnp.float32) + active * gate[:, None, None, :]).astype(jnp.bfloat16)
    return out, (mixed, pooled, squeezed, hidden, gate)


def silu_slope(value):
    sig = jax.nn.sigmoid(value)
    return sig * (1.0 + value * (1.0 - sig))


def pull_back(cotangent, kernel, reduce_w, expand_w, held):
    mixed, pooled, squeezed, hidden, gate = held
    images, side_h, side_w, channels = mixed.shape
    grad = cotangent.astype(jnp.float32)
    d_gate = jnp.sum(grad * jax.nn.silu(mixed), axis=(1, 2)) * gate * (1.0 - gate)
    d_gate = d_gate.astype(jnp.bfloat16)
    d_hidden = lax.dot_general(
        d_gate, expand_w, (((1,), (1,)), ((), ())), preferred_element_type=jnp.float32
    )
    d_squeezed = (d_hidden * silu_slope(squeezed)).astype(jnp.bfloat16)
    d_pooled = lax.dot_general(
        d_squeezed, reduce_w, (((1,), (1,)), ((), ())), preferred_element_type=jnp.float32
    ) / (side_h * side_w)
    d_mixed = (grad * gate[:, None, None, :] + d_pooled[:, None, None, :]) * silu_slope(mixed)
    d_mixed = d_mixed.astype(jnp.bfloat16).reshape(-1, channels)
    d_columns = lax.dot_general(
        d_mixed, kernel, (((1,), (1,)), ((), ())), preferred_element_type=jnp.float32
    ).astype(jnp.bfloat16)
    d_columns = d_columns.reshape(images, side_h, side_w, 9, channels)
    total = grad
    for tap in range(9):
        row, col = tap // 3 - 1, tap % 3 - 1
        piece = d_columns[:, :, :, tap].astype(jnp.float32)
        piece = lax.pad(
            piece,
            jnp.float32(0),
            ((0, 0, 0), (row, -row, 0), (col, -col, 0), (0, 0, 0)),
        )
        total = total + piece
    return total.astype(jnp.bfloat16), (d_mixed, d_gate, d_squeezed)


def transposed_dot(left, right):
    return lax.dot_general(
        left, right, (((0,), (0,)), ((), ())), preferred_element_type=jnp.float32
    ).astype(jnp.bfloat16)


def per_device(student_in, teacher_in, out_grad, student_params, teacher_params):
    shape = student_in.shape
    channels = shape[-1]
    flat = (shape[0] * shape[1],) + shape[2:]
    sections = lax.axis_size("segment")
    section = lax.axis_index("segment")
    student_own = student_params.reshape(-1, channels)
    teacher_own = teacher_params.reshape(-1, channels)
    student_rows = lax.all_gather(student_own.astype(jnp.bfloat16), "dp", axis=0, tiled=True)
    student_rows, teacher_own = lax.optimization_barrier((student_rows, teacher_own))
    teacher_rows = lax.all_gather(teacher_own.astype(jnp.bfloat16), "dp", axis=0, tiled=True)
    student_w = split_rows(student_rows, channels, SE)

    current = student_in.reshape(flat)
    for step in range(sections):
        result, held = forward(current, *student_w)
        if step + 1 < sections:
            got = shift(result, "segment", 1)
            current = jnp.where(section == step + 1, got, current)

    grad = out_grad.reshape(flat)
    for step in range(sections):
        result, parts = pull_back(grad, *student_w, held)
        if step + 1 < sections:
            got = shift(result, "segment", -1)
            grad = jnp.where(section == sections - 2 - step, got, grad)
    input_grads = result

    d_mixed, d_gate, d_squeezed = parts
    _, pooled, _, hidden, _ = held
    rows = jnp.concatenate(
        [
            transposed_dot(unfold(current), d_mixed),
            transposed_dot(pooled, d_squeezed).reshape(-1, channels),
            transposed_dot(hidden, d_gate).reshape(-1, channels),
        ],
        axis=0,
    )
    grad_own = lax.psum_scatter(rows, "dp", scatter_dimension=0, tiled=True).astype(jnp.float32)

    teacher_w = split_rows(teacher_rows, channels, SE)
    teacher_now, _ = lax.optimization_barrier((teacher_in.reshape(flat), rows))
    for step in range(sections):
        teacher_out, _ = forward(teacher_now, *teacher_w)
        if step + 1 < sections:
            got = shift(teacher_out, "segment", 1)
            teacher_now = jnp.where(section == step + 1, got, teacher_now)

    grad_shard = grad_own.reshape(student_params.shape)
    teacher_new = ema_keep * teacher_params + (1.0 - ema_keep) * (
        student_params - step_rate * grad_shard
    )
    return (
        teacher_out.reshape((1,) + shape),
        input_grads.reshape((1,) + shape),
        grad_shard,
        teacher_new,
    )


def solution(mesh):
    placed = (
        P(None, "dp", None, None, None),
        P(None, "dp", None, None, None),
        P(None, "dp", None, None, None),
        P("segment", "dp"),
        P("segment", "dp"),
    )
    return jax.shard_map(
        per_device,
        mesh=mesh,
        in_specs=placed,
        out_specs=(
            P("segment", None, "dp", None, None, None),
            P("segment", None, "dp", None, None, None),
            P("segment", "dp"),
            P("segment", "dp"),
        ),
        check_vma=False,
    )
```

```python
import jax
import jax.numpy as jnp
from jax import lax
from jax.experimental import pallas as pl
from jax.experimental.pallas import tpu as pltpu
from jax.sharding import PartitionSpec as P

SE = 256


ema_keep = 0.99
step_rate = 0.001


def hop(array, axis, source, target):
    return lax.ppermute(array, axis, [(source, target)])


def split_rows(rows, channels, squeeze):
    taps = 9 * channels
    reduce_w = rows[taps : taps + squeeze].reshape(channels, squeeze)
    expand_w = rows[taps + squeeze :].reshape(squeeze, channels)
    return (rows, reduce_w, expand_w)


def whole(shape):
    return pl.BlockSpec(shape, lambda *step: (0,) * len(shape))


def params(mega):
    return pltpu.CompilerParams(vmem_limit_bytes=mega * 1024 * 1024)


def to_matrix(flat, channels):
    lanes = 128
    parts = channels // lanes
    rows = flat.shape[1] // channels

    def body(flat_ref, out_ref):
        for part in range(parts):
            piece = flat_ref[pl.ds(part, rows, stride=parts), :]
            out_ref[:, part * lanes : (part + 1) * lanes] = piece.astype(jnp.bfloat16)

    return pl.pallas_call(
        body,
        out_shape=jax.ShapeDtypeStruct((rows, channels), jnp.bfloat16),
        compiler_params=params(24),
        cost_estimate=pl.CostEstimate(
            flops=rows * channels, bytes_accessed=6 * rows * channels, transcendentals=0
        ),
    )(flat.reshape(rows * parts, lanes))


def finish(grad_own, student_params, teacher_params):
    rows, channels = grad_own.shape
    lanes = 128
    parts = channels // lanes

    def body(grad_ref, student_ref, teacher_ref, flat_ref, new_ref):
        for part in range(parts):
            piece = grad_ref[:, part * lanes : (part + 1) * lanes].astype(jnp.float32)
            here = pl.ds(part, rows, stride=parts)
            flat_ref[here, :] = piece
            stepped = student_ref[here, :] - step_rate * piece
            new_ref[here, :] = ema_keep * teacher_ref[here, :] + (1.0 - ema_keep) * stepped

    flat_shape = jax.ShapeDtypeStruct((rows * parts, lanes), jnp.float32)
    flat, new = pl.pallas_call(
        body,
        out_shape=(flat_shape, flat_shape),
        compiler_params=params(24),
        cost_estimate=pl.CostEstimate(
            flops=5 * rows * channels, bytes_accessed=18 * rows * channels, transcendentals=0
        ),
    )(
        grad_own,
        student_params.reshape(rows * parts, lanes),
        teacher_params.reshape(rows * parts, lanes),
    )
    return flat.reshape(student_params.shape), new.reshape(teacher_params.shape)


def spread(values, shifted, side, count):
    line = side * count
    channels = values.shape[-1]
    edge = jnp.zeros((line, channels), jnp.bfloat16)
    grid = values.reshape(side, side, count, channels)
    blank = jnp.zeros((side, 1, count, channels), jnp.float32)
    versions = (
        jnp.concatenate([blank, grid[:, : side - 1]], axis=1),
        grid,
        jnp.concatenate([grid[:, 1:], blank], axis=1),
    )
    for col in range(3):
        shifted[col, :line, :] = edge
        shifted[col, line : line + side * line, :] = (
            versions[col].reshape(side * line, channels).astype(jnp.bfloat16)
        )
        shifted[col, line + side * line :, :] = edge


def silu(value):
    return value / (1.0 + jnp.exp(-value))


def sigmoid(value):
    return 1.0 / (1.0 + jnp.exp(-value))


def silu_slope(value):
    sig = sigmoid(value)
    return sig * (1.0 + value * (1.0 - sig))


def forward(images, rows, reduce_w, expand_w, side, count):
    area, channels = images.shape
    squeeze = reduce_w.shape[1]
    line = side * count

    def body(x_ref, kernel_ref, red_ref, exp_ref, out_ref, mixed_ref, pool_ref, sq_ref, hid_ref, gate_ref, shifted):
        step = pl.program_id(0)

        @pl.when(step == 0)
        def _():
            spread(x_ref[...].astype(jnp.float32), shifted, side, count)
            mixed_ref[...] = jnp.zeros_like(mixed_ref)

        here = pl.ds(pl.multiple_of(step * line, line), area)
        total = mixed_ref[...]
        for col in range(3):
            total += jnp.dot(
                shifted[col, here, :],
                kernel_ref[col * channels : (col + 1) * channels, :],
                preferred_element_type=jnp.float32,
            )
        mixed_ref[...] = total

        @pl.when(step == 2)
        def _():
            active = silu(mixed_ref[...]).reshape(side * side, count, channels)
            pooled = (jnp.sum(active, axis=0) / (side * side)).astype(jnp.bfloat16)
            squeezed = jnp.dot(pooled, red_ref[...], preferred_element_type=jnp.float32)
            hidden = silu(squeezed).astype(jnp.bfloat16)
            gate = sigmoid(jnp.dot(hidden, exp_ref[...], preferred_element_type=jnp.float32))
            x = x_ref[...].astype(jnp.float32).reshape(active.shape)
            out = x + active * gate[None]
            out_ref[...] = out.reshape(area, channels).astype(jnp.bfloat16)
            pool_ref[...] = pooled.astype(jnp.float32)
            sq_ref[...] = squeezed
            hid_ref[...] = hidden.astype(jnp.float32)
            gate_ref[...] = gate

    shapes = (
        ((area, channels), jnp.bfloat16),
        ((area, channels), jnp.float32),
        ((count, channels), jnp.float32),
        ((count, squeeze), jnp.float32),
        ((count, squeeze), jnp.float32),
        ((count, channels), jnp.float32),
    )
    out, *held = pl.pallas_call(
        body,
        grid=(3,),
        in_specs=[
            whole(images.shape),
            pl.BlockSpec((3 * channels, channels), lambda step: (step, 0)),
            whole(reduce_w.shape),
            whole(expand_w.shape),
        ],
        out_specs=[whole(shape) for shape, _ in shapes],
        out_shape=[jax.ShapeDtypeStruct(*shape) for shape in shapes],
        scratch_shapes=[pltpu.VMEM((3, area + 2 * line, channels), jnp.bfloat16)],
        compiler_params=params(40),
        cost_estimate=pl.CostEstimate(
            flops=18 * area * channels * channels, bytes_accessed=8000000, transcendentals=area * channels
        ),
    )(images, rows, reduce_w, expand_w)
    return out, held


def pull_back(cotangent, rows, reduce_w, expand_w, held, side, count):
    mixed, _, squeezed, _, gate = held
    area, channels = cotangent.shape
    squeeze = reduce_w.shape[1]
    line = side * count

    def body(g_ref, mixed_ref, sq_ref, gate_ref, kernel_ref, red_ref, exp_ref, dx_ref, dm_ref, dg_ref, ds_ref, shifted, total_ref):
        step = pl.program_id(0)

        @pl.when(step == 0)
        def _():
            grad = g_ref[...].astype(jnp.float32)
            total_ref[...] = grad
            grad = grad.reshape(side * side, count, channels)
            value = mixed_ref[...].reshape(grad.shape)
            gate_val = gate_ref[...]
            sig = sigmoid(value)
            d_gate = jnp.sum(grad * value * sig, axis=0) * gate_val * (1.0 - gate_val)
            d_hidden = lax.dot_general(
                d_gate.astype(jnp.bfloat16),
                exp_ref[...],
                (((1,), (1,)), ((), ())),
                preferred_element_type=jnp.float32,
            )
            d_squeezed = d_hidden * silu_slope(sq_ref[...])
            d_pooled = lax.dot_general(
                d_squeezed.astype(jnp.bfloat16),
                red_ref[...],
                (((1,), (1,)), ((), ())),
                preferred_element_type=jnp.float32,
            ) / (side * side)
            slope = sig * (1.0 + value * (1.0 - sig))
            d_mixed = (grad * gate_val[None] + d_pooled[None]) * slope
            d_mixed = d_mixed.reshape(area, channels)
            dm_ref[...] = d_mixed.astype(jnp.bfloat16)
            dg_ref[...] = d_gate
            ds_ref[...] = d_squeezed
            spread(d_mixed, shifted, side, count)

        here = pl.ds(pl.multiple_of((2 - step) * line, line), area)
        total = total_ref[...]
        for col in range(3):
            total += lax.dot_general(
                shifted[2 - col, here, :],
                kernel_ref[col * channels : (col + 1) * channels, :],
                (((1,), (1,)), ((), ())),
                preferred_element_type=jnp.float32,
            )
        total_ref[...] = total

        @pl.when(step == 2)
        def _():
            dx_ref[...] = total_ref[...].astype(jnp.bfloat16)

    shapes = (
        ((area, channels), jnp.bfloat16),
        ((area, channels), jnp.bfloat16),
        ((count, channels), jnp.float32),
        ((count, squeeze), jnp.float32),
    )
    d_in, *parts = pl.pallas_call(
        body,
        grid=(3,),
        in_specs=[
            whole(cotangent.shape),
            whole(mixed.shape),
            whole(squeezed.shape),
            whole(gate.shape),
            pl.BlockSpec((3 * channels, channels), lambda step: (step, 0)),
            whole(reduce_w.shape),
            whole(expand_w.shape),
        ],
        out_specs=[whole(shape) for shape, _ in shapes],
        out_shape=[jax.ShapeDtypeStruct(*shape) for shape in shapes],
        scratch_shapes=[
            pltpu.VMEM((3, area + 2 * line, channels), jnp.bfloat16),
            pltpu.VMEM((area, channels), jnp.float32),
        ],
        compiler_params=params(40),
        cost_estimate=pl.CostEstimate(
            flops=18 * area * channels * channels, bytes_accessed=9000000, transcendentals=area * channels
        ),
    )(cotangent, mixed, squeezed, gate, rows, reduce_w, expand_w)
    return d_in, parts


def weight_rows(images, d_mixed, tail, side, count):
    area, channels = images.shape
    line = side * count

    def body(x_ref, dm_ref, tail_ref, out_ref, shifted):
        step = pl.program_id(0)

        @pl.when(step == 0)
        def _():
            spread(x_ref[...].astype(jnp.float32), shifted, side, count)

        @pl.when(step < 9)
        def _():
            here = pl.ds(pl.multiple_of((step // 3) * line, line), area)
            out_ref[...] = lax.dot_general(
                shifted[step % 3, here, :],
                dm_ref[...],
                (((0,), (0,)), ((), ())),
                preferred_element_type=jnp.float32,
            ).astype(jnp.bfloat16)

        @pl.when(step == 9)
        def _():
            out_ref[...] = tail_ref[...]

    return pl.pallas_call(
        body,
        grid=(10,),
        in_specs=[whole(images.shape), whole(d_mixed.shape), whole(tail.shape)],
        out_specs=pl.BlockSpec((channels, channels), lambda step: (step, 0)),
        out_shape=jax.ShapeDtypeStruct((10 * channels, channels), jnp.bfloat16),
        scratch_shapes=[pltpu.VMEM((3, area + 2 * line, channels), jnp.bfloat16)],
        compiler_params=params(40),
        cost_estimate=pl.CostEstimate(
            flops=18 * area * channels * channels, bytes_accessed=7000000, transcendentals=0
        ),
    )(images, d_mixed, tail)


def transposed_dot(left, right):
    return lax.dot_general(
        left.astype(jnp.bfloat16),
        right.astype(jnp.bfloat16),
        (((0,), (0,)), ((), ())),
        preferred_element_type=jnp.float32,
    ).astype(jnp.bfloat16)


def per_device(student_in, teacher_in, out_grad, student_params, teacher_params):
    shape = student_in.shape
    channels, side, count = shape[-1], shape[2], shape[0] * shape[1]
    sections = lax.axis_size("segment")
    section = lax.axis_index("segment")

    def pack(array):
        array = array.reshape((count, side, side, channels)).transpose(1, 2, 0, 3)
        return array.reshape(side * side * count, channels)

    def unpack(array):
        array = array.reshape((side, side, count, channels)).transpose(2, 0, 1, 3)
        return array.reshape((1,) + shape)

    student_own = to_matrix(student_params, channels)
    student_rows = lax.all_gather(student_own, "dp", axis=0, tiled=True)
    teacher_own = to_matrix(teacher_params, channels)
    student_rows, teacher_own = lax.optimization_barrier((student_rows, teacher_own))
    teacher_rows = lax.all_gather(teacher_own, "dp", axis=0, tiled=True)
    student_w = split_rows(student_rows, channels, SE)

    current = pack(student_in)
    for step in range(sections):
        result, held = forward(current, *student_w, side, count)
        if step + 1 < sections:
            got = hop(result, "segment", step, step + 1)
            current = jnp.where(section == step + 1, got, current)

    grad = pack(out_grad)
    for step in range(sections):
        if step == sections // 2:
            grad, teacher_rows = lax.optimization_barrier((grad, teacher_rows))
        result, parts = pull_back(grad, *student_w, held, side, count)
        if step + 1 < sections:
            got = hop(result, "segment", sections - 1 - step, sections - 2 - step)
            grad = jnp.where(section == sections - 2 - step, got, grad)
    input_grads = result

    d_mixed, d_gate, d_squeezed = parts
    _, pooled, _, hidden, _ = held
    tail = jnp.concatenate(
        [
            transposed_dot(pooled, d_squeezed).reshape(-1, channels),
            transposed_dot(hidden, d_gate).reshape(-1, channels),
        ],
        axis=0,
    )
    rows = weight_rows(current, d_mixed, tail, side, count)
    grad_own = lax.psum_scatter(rows, "dp", scatter_dimension=0, tiled=True)

    teacher_w = split_rows(teacher_rows, channels, SE)
    teacher_now, _ = lax.optimization_barrier((pack(teacher_in), rows))
    for step in range(sections):
        teacher_out, _ = forward(teacher_now, *teacher_w, side, count)
        if step + 1 < sections:
            got = hop(teacher_out, "segment", step, step + 1)
            teacher_now = jnp.where(section == step + 1, got, teacher_now)

    grad_shard, teacher_new = finish(grad_own, student_params, teacher_params)
    return (unpack(teacher_out), unpack(input_grads), grad_shard, teacher_new)


def solution(mesh):
    placed = (
        P(None, "dp", None, None, None),
        P(None, "dp", None, None, None),
        P(None, "dp", None, None, None),
        P("segment", "dp"),
        P("segment", "dp"),
    )
    return jax.shard_map(
        per_device,
        mesh=mesh,
        in_specs=placed,
        out_specs=(
            P("segment", None, "dp", None, None, None),
            P("segment", None, "dp", None, None, None),
            P("segment", "dp"),
            P("segment", "dp"),
        ),
        check_vma=False,
    )
```

```python
import jax
import jax.numpy as jnp
from jax import lax
from jax.experimental import pallas as pl
from jax.experimental.pallas import tpu as pltpu
from jax.sharding import PartitionSpec as P

SE = 256


ema_keep = 0.99
step_rate = 0.001


def hop(array, axis, source, target):
    return lax.ppermute(array, axis, [(source, target)])


def split_rows(rows, channels, squeeze):
    taps = 9 * channels
    reduce_w = rows[taps : taps + squeeze].reshape(channels, squeeze)
    expand_w = rows[taps + squeeze :].reshape(squeeze, channels)
    return (rows, reduce_w, expand_w)


def whole(shape):
    return pl.BlockSpec(shape, lambda *step: (0,) * len(shape))


def params(mega):
    return pltpu.CompilerParams(vmem_limit_bytes=mega * 1024 * 1024)


def to_matrix(flat, channels):
    lanes = 128
    parts = channels // lanes
    rows = flat.shape[1] // channels

    def body(flat_ref, out_ref):
        for part in range(parts):
            piece = flat_ref[pl.ds(part, rows, stride=parts), :]
            out_ref[:, part * lanes : (part + 1) * lanes] = piece.astype(jnp.bfloat16)

    return pl.pallas_call(
        body,
        out_shape=jax.ShapeDtypeStruct((rows, channels), jnp.bfloat16),
        compiler_params=params(24),
        cost_estimate=pl.CostEstimate(
            flops=rows * channels, bytes_accessed=6 * rows * channels, transcendentals=0
        ),
    )(flat.reshape(rows * parts, lanes))


def finish(grad_own, student_params, teacher_params):
    rows, channels = grad_own.shape
    lanes = 128
    parts = channels // lanes

    def body(grad_ref, student_ref, teacher_ref, flat_ref, new_ref):
        for part in range(parts):
            piece = grad_ref[:, part * lanes : (part + 1) * lanes].astype(jnp.float32)
            here = pl.ds(part, rows, stride=parts)
            flat_ref[here, :] = piece
            stepped = student_ref[here, :] - step_rate * piece
            new_ref[here, :] = ema_keep * teacher_ref[here, :] + (1.0 - ema_keep) * stepped

    flat_shape = jax.ShapeDtypeStruct((rows * parts, lanes), jnp.float32)
    flat, new = pl.pallas_call(
        body,
        out_shape=(flat_shape, flat_shape),
        compiler_params=params(24),
        cost_estimate=pl.CostEstimate(
            flops=5 * rows * channels, bytes_accessed=18 * rows * channels, transcendentals=0
        ),
    )(
        grad_own,
        student_params.reshape(rows * parts, lanes),
        teacher_params.reshape(rows * parts, lanes),
    )
    return flat.reshape(student_params.shape), new.reshape(teacher_params.shape)


def spread(values, shifted, side, count):
    line = side * count
    channels = values.shape[-1]
    edge = jnp.zeros((line, channels), jnp.bfloat16)
    grid = values.reshape(side, side, count, channels)
    blank = jnp.zeros((side, 1, count, channels), jnp.float32)
    versions = (
        jnp.concatenate([blank, grid[:, : side - 1]], axis=1),
        grid,
        jnp.concatenate([grid[:, 1:], blank], axis=1),
    )
    for col in range(3):
        shifted[col, :line, :] = edge
        shifted[col, line : line + side * line, :] = (
            versions[col].reshape(side * line, channels).astype(jnp.bfloat16)
        )
        shifted[col, line + side * line :, :] = edge


def silu(value):
    return value / (1.0 + jnp.exp(-value))


def sigmoid(value):
    return 1.0 / (1.0 + jnp.exp(-value))


def silu_slope(value):
    sig = sigmoid(value)
    return sig * (1.0 + value * (1.0 - sig))


def forward(images, rows, reduce_w, expand_w, side, count):
    area, channels = images.shape
    squeeze = reduce_w.shape[1]
    line = side * count

    def body(x_ref, kernel_ref, red_ref, exp_ref, out_ref, mixed_ref, pool_ref, sq_ref, hid_ref, gate_ref, shifted):
        step = pl.program_id(0)

        @pl.when(step == 0)
        def _():
            spread(x_ref[...].astype(jnp.float32), shifted, side, count)
            mixed_ref[...] = jnp.zeros_like(mixed_ref)

        here = pl.ds(pl.multiple_of(step * line, line), area)
        total = mixed_ref[...]
        for col in range(3):
            total += jnp.dot(
                shifted[col, here, :],
                kernel_ref[col * channels : (col + 1) * channels, :],
                preferred_element_type=jnp.float32,
            )
        mixed_ref[...] = total

        @pl.when(step == 2)
        def _():
            active = silu(mixed_ref[...]).reshape(side * side, count, channels)
            pooled = (jnp.sum(active, axis=0) / (side * side)).astype(jnp.bfloat16)
            squeezed = jnp.dot(pooled, red_ref[...], preferred_element_type=jnp.float32)
            hidden = silu(squeezed).astype(jnp.bfloat16)
            gate = sigmoid(jnp.dot(hidden, exp_ref[...], preferred_element_type=jnp.float32))
            x = x_ref[...].astype(jnp.float32).reshape(active.shape)
            out = x + active * gate[None]
            out_ref[...] = out.reshape(area, channels).astype(jnp.bfloat16)
            pool_ref[...] = pooled.astype(jnp.float32)
            sq_ref[...] = squeezed
            hid_ref[...] = hidden.astype(jnp.float32)
            gate_ref[...] = gate

    shapes = (
        ((area, channels), jnp.bfloat16),
        ((area, channels), jnp.float32),
        ((count, channels), jnp.float32),
        ((count, squeeze), jnp.float32),
        ((count, squeeze), jnp.float32),
        ((count, channels), jnp.float32),
    )
    out, *held = pl.pallas_call(
        body,
        grid=(3,),
        in_specs=[
            whole(images.shape),
            pl.BlockSpec((3 * channels, channels), lambda step: (step, 0)),
            whole(reduce_w.shape),
            whole(expand_w.shape),
        ],
        out_specs=[whole(shape) for shape, _ in shapes],
        out_shape=[jax.ShapeDtypeStruct(*shape) for shape in shapes],
        scratch_shapes=[pltpu.VMEM((3, area + 2 * line, channels), jnp.bfloat16)],
        compiler_params=params(40),
        cost_estimate=pl.CostEstimate(
            flops=18 * area * channels * channels, bytes_accessed=8000000, transcendentals=area * channels
        ),
    )(images, rows, reduce_w, expand_w)
    return out, held


def pull_back(cotangent, rows, reduce_w, expand_w, held, side, count):
    mixed, _, squeezed, _, gate = held
    area, channels = cotangent.shape
    squeeze = reduce_w.shape[1]
    line = side * count

    def body(g_ref, mixed_ref, sq_ref, gate_ref, kernel_ref, red_ref, exp_ref, dx_ref, dm_ref, dg_ref, ds_ref, shifted, total_ref):
        step = pl.program_id(0)

        @pl.when(step == 0)
        def _():
            grad = g_ref[...].astype(jnp.float32)
            total_ref[...] = grad
            grad = grad.reshape(side * side, count, channels)
            value = mixed_ref[...].reshape(grad.shape)
            gate_val = gate_ref[...]
            sig = sigmoid(value)
            d_gate = jnp.sum(grad * value * sig, axis=0) * gate_val * (1.0 - gate_val)
            d_hidden = lax.dot_general(
                d_gate.astype(jnp.bfloat16),
                exp_ref[...],
                (((1,), (1,)), ((), ())),
                preferred_element_type=jnp.float32,
            )
            d_squeezed = d_hidden * silu_slope(sq_ref[...])
            d_pooled = lax.dot_general(
                d_squeezed.astype(jnp.bfloat16),
                red_ref[...],
                (((1,), (1,)), ((), ())),
                preferred_element_type=jnp.float32,
            ) / (side * side)
            slope = sig * (1.0 + value * (1.0 - sig))
            d_mixed = (grad * gate_val[None] + d_pooled[None]) * slope
            d_mixed = d_mixed.reshape(area, channels)
            dm_ref[...] = d_mixed.astype(jnp.bfloat16)
            dg_ref[...] = d_gate
            ds_ref[...] = d_squeezed
            spread(d_mixed, shifted, side, count)

        here = pl.ds(pl.multiple_of((2 - step) * line, line), area)
        total = total_ref[...]
        for col in range(3):
            total += lax.dot_general(
                shifted[2 - col, here, :],
                kernel_ref[col * channels : (col + 1) * channels, :],
                (((1,), (1,)), ((), ())),
                preferred_element_type=jnp.float32,
            )
        total_ref[...] = total

        @pl.when(step == 2)
        def _():
            dx_ref[...] = total_ref[...].astype(jnp.bfloat16)

    shapes = (
        ((area, channels), jnp.bfloat16),
        ((area, channels), jnp.bfloat16),
        ((count, channels), jnp.float32),
        ((count, squeeze), jnp.float32),
    )
    d_in, *parts = pl.pallas_call(
        body,
        grid=(3,),
        in_specs=[
            whole(cotangent.shape),
            whole(mixed.shape),
            whole(squeezed.shape),
            whole(gate.shape),
            pl.BlockSpec((3 * channels, channels), lambda step: (step, 0)),
            whole(reduce_w.shape),
            whole(expand_w.shape),
        ],
        out_specs=[whole(shape) for shape, _ in shapes],
        out_shape=[jax.ShapeDtypeStruct(*shape) for shape in shapes],
        scratch_shapes=[
            pltpu.VMEM((3, area + 2 * line, channels), jnp.bfloat16),
            pltpu.VMEM((area, channels), jnp.float32),
        ],
        compiler_params=params(40),
        cost_estimate=pl.CostEstimate(
            flops=18 * area * channels * channels, bytes_accessed=9000000, transcendentals=area * channels
        ),
    )(cotangent, mixed, squeezed, gate, rows, reduce_w, expand_w)
    return d_in, parts


def weight_rows(images, d_mixed, tail, side, count):
    area, channels = images.shape
    line = side * count

    def body(x_ref, dm_ref, tail_ref, out_ref, shifted):
        step = pl.program_id(0)

        @pl.when(step == 0)
        def _():
            spread(x_ref[...].astype(jnp.float32), shifted, side, count)

        @pl.when(step < 9)
        def _():
            here = pl.ds(pl.multiple_of((step // 3) * line, line), area)
            out_ref[...] = lax.dot_general(
                shifted[step % 3, here, :],
                dm_ref[...],
                (((0,), (0,)), ((), ())),
                preferred_element_type=jnp.float32,
            ).astype(jnp.bfloat16)

        @pl.when(step == 9)
        def _():
            out_ref[...] = tail_ref[...]

    return pl.pallas_call(
        body,
        grid=(10,),
        in_specs=[whole(images.shape), whole(d_mixed.shape), whole(tail.shape)],
        out_specs=pl.BlockSpec((channels, channels), lambda step: (step, 0)),
        out_shape=jax.ShapeDtypeStruct((10 * channels, channels), jnp.bfloat16),
        scratch_shapes=[pltpu.VMEM((3, area + 2 * line, channels), jnp.bfloat16)],
        compiler_params=params(40),
        cost_estimate=pl.CostEstimate(
            flops=18 * area * channels * channels, bytes_accessed=7000000, transcendentals=0
        ),
    )(images, d_mixed, tail)


def ring_sizes():
    across = max(lax.axis_size("segment") // 2, 1)
    return across, lax.axis_size("dp") // across


def ring_place(spot):
    across, along = ring_sizes()
    if across == 1:
        return spot
    away = (spot // along + across - 1) // across
    rest = away * (spot - along)
    row, step = rest // (across - 1), rest % (across - 1)
    x = 1 + step + (row % 2) * (across - 2 - 2 * step)
    return (1 - away) * spot * across + away * ((along - 1 - row) * across + x)


def ring_spot(place):
    across, along = ring_sizes()
    if across == 1:
        return place
    x, z = place % across, place // across
    away = (x + across - 1) // across
    row = along - 1 - z
    step = x - 1 + (row % 2) * (across - 2 - 2 * (x - 1))
    return (1 - away) * z + away * (along + row * (across - 1) + step)


def ring_gather(own):
    peers = lax.axis_size("dp")
    depth, channels = own.shape
    half = depth // 2
    pieces = 2 if half % 32 == 0 else 1
    part = half // pieces
    lanes = [(way, piece) for piece in range(pieces) for way in range(2)]

    def body(own_ref, out_ref, local_sem, send_sem, recv_sem):
        me = lax.axis_index("dp")
        spot = ring_spot(me)
        sides = (ring_place((spot + 1) % peers), ring_place((spot + peers - 1) % peers))
        barrier = pltpu.get_barrier_semaphore()
        for side in sides:
            pl.semaphore_signal(
                barrier, inc=1, device_id={"dp": side}, device_id_type=pl.DeviceIdType.MESH
            )
        pl.semaphore_wait(barrier, 2)

        def copy(step, way, piece):
            spot_of = spot + peers - step if way == 0 else spot + step
            start = way * half + piece * part
            block = pl.multiple_of(ring_place(spot_of % peers) * depth, 16)
            landing = out_ref.at[pl.ds(block + start, part)]
            source = own_ref.at[pl.ds(start, part)] if step == 0 else landing
            return pltpu.make_async_remote_copy(
                src_ref=source,
                dst_ref=landing,
                send_sem=send_sem.at[way, piece, step],
                recv_sem=recv_sem.at[way, piece, step],
                device_id={"dp": sides[way]},
                device_id_type=pl.DeviceIdType.MESH,
            )

        copies = {}
        for step in range(peers - 1):
            for way, piece in lanes:
                if step > 0:
                    copies[step - 1, way, piece].wait_recv()
                copies[step, way, piece] = copy(step, way, piece)
                copies[step, way, piece].start()
            if step == 0:
                mine = pltpu.make_async_copy(
                    own_ref, out_ref.at[pl.ds(pl.multiple_of(me * depth, 16), depth)], local_sem
                )
                mine.start()
        for way, piece in lanes:
            copies[peers - 2, way, piece].wait_recv()
        for key in copies:
            copies[key].wait_send()
        mine.wait()

    return pl.pallas_call(
        body,
        in_specs=[pl.BlockSpec(memory_space=pl.ANY)],
        out_specs=pl.BlockSpec(memory_space=pl.ANY),
        out_shape=jax.ShapeDtypeStruct((peers * depth, channels), own.dtype),
        scratch_shapes=[
            pltpu.SemaphoreType.DMA,
            pltpu.SemaphoreType.DMA((2, pieces, peers - 1)),
            pltpu.SemaphoreType.DMA((2, pieces, peers - 1)),
        ],
        compiler_params=pltpu.CompilerParams(collective_id=0, has_side_effects=True),
        cost_estimate=pl.CostEstimate(
            flops=0, bytes_accessed=4 * peers * depth * channels, transcendentals=0
        ),
    )(own)


def ring_scatter(rows):
    peers = lax.axis_size("dp")
    depth = rows.shape[0] // peers
    half = depth // 2
    spot = ring_spot(lax.axis_index("dp"))
    order = [ring_place(at) for at in range(peers)]
    pairs = (
        [(order[at], order[(at + 1) % peers]) for at in range(peers)],
        [(order[(at + 1) % peers], order[at]) for at in range(peers)],
    )

    def term(way, step):
        spot_of = spot + 2 * peers - 1 - step if way == 0 else spot + 1 + step
        start = ring_place(spot_of % peers) * depth + way * half
        return lax.dynamic_slice_in_dim(rows, start, half, 0)

    moving = [term(way, 0) for way in range(2)]
    for step in range(peers - 1):
        for way in range(2):
            got = lax.ppermute(moving[way], "dp", pairs[way])
            total = got.astype(jnp.float32) + term(way, step + 1).astype(jnp.float32)
            moving[way] = total if step == peers - 2 else total.astype(jnp.bfloat16)
    return jnp.concatenate(moving, axis=0)


def transposed_dot(left, right):
    return lax.dot_general(
        left.astype(jnp.bfloat16),
        right.astype(jnp.bfloat16),
        (((0,), (0,)), ((), ())),
        preferred_element_type=jnp.float32,
    ).astype(jnp.bfloat16)


def per_device(student_in, teacher_in, out_grad, student_params, teacher_params):
    shape = student_in.shape
    channels, side, count = shape[-1], shape[2], shape[0] * shape[1]
    sections = lax.axis_size("segment")
    section = lax.axis_index("segment")

    def pack(array):
        array = array.reshape((count, side, side, channels)).transpose(1, 2, 0, 3)
        return array.reshape(side * side * count, channels)

    def unpack(array):
        array = array.reshape((side, side, count, channels)).transpose(2, 0, 1, 3)
        return array.reshape((1,) + shape)

    student_own = to_matrix(student_params, channels)
    student_rows = ring_gather(student_own)
    teacher_own = to_matrix(teacher_params, channels)
    student_rows, teacher_own = lax.optimization_barrier((student_rows, teacher_own))
    teacher_rows = lax.all_gather(teacher_own, "dp", axis=0, tiled=True)
    student_w = split_rows(student_rows, channels, SE)

    current = pack(student_in)
    for step in range(sections):
        result, held = forward(current, *student_w, side, count)
        if step + 1 < sections:
            got = hop(result, "segment", step, step + 1)
            current = jnp.where(section == step + 1, got, current)

    grad = pack(out_grad)
    for step in range(sections):
        result, parts = pull_back(grad, *student_w, held, side, count)
        if step + 1 < sections:
            got = hop(result, "segment", sections - 1 - step, sections - 2 - step)
            grad = jnp.where(section == sections - 2 - step, got, grad)
    input_grads = result
    parts[0], teacher_rows = lax.optimization_barrier((parts[0], teacher_rows))

    d_mixed, d_gate, d_squeezed = parts
    _, pooled, _, hidden, _ = held
    tail = jnp.concatenate(
        [
            transposed_dot(pooled, d_squeezed).reshape(-1, channels),
            transposed_dot(hidden, d_gate).reshape(-1, channels),
        ],
        axis=0,
    )
    rows = weight_rows(current, d_mixed, tail, side, count)
    grad_own = ring_scatter(rows)

    teacher_w = split_rows(teacher_rows, channels, SE)
    teacher_now, _ = lax.optimization_barrier((pack(teacher_in), rows))
    for step in range(sections):
        teacher_out, _ = forward(teacher_now, *teacher_w, side, count)
        if step + 1 < sections:
            got = hop(teacher_out, "segment", step, step + 1)
            teacher_now = jnp.where(section == step + 1, got, teacher_now)

    grad_shard, teacher_new = finish(grad_own, student_params, teacher_params)
    return (unpack(teacher_out), unpack(input_grads), grad_shard, teacher_new)


def solution(mesh):
    placed = (
        P(None, "dp", None, None, None),
        P(None, "dp", None, None, None),
        P(None, "dp", None, None, None),
        P("segment", "dp"),
        P("segment", "dp"),
    )
    return jax.shard_map(
        per_device,
        mesh=mesh,
        in_specs=placed,
        out_specs=(
            P("segment", None, "dp", None, None, None),
            P("segment", None, "dp", None, None, None),
            P("segment", "dp"),
            P("segment", "dp"),
        ),
        check_vma=False,
    )
```
